32 devices in a mesh: shard: 2 (over core), context: 4 (over y, x), tensor: 4 (over z).
Axes of the slice: x: 2, y: 2, z: 4, core: 2. Of those that a mesh axis runs over, the one named last changes fastest.
Arguments:
- tokens: bfloat16 [16384, 1024], P(('shard', 'context', 'tensor')), may hold values from -6 to 6
- segments: int32 [8, 2048], P(('shard', 'tensor')), may hold values from 0 to 4, as said below
- attention_gain: float32 [1024], replicated, may hold values from 0.25 to 1.75
- query_weight: bfloat16 [1024, 1024], P(('shard', 'context'), 'tensor'), may hold values from -0.1875 to 0.1875
- key_weight: bfloat16 [1024, 512], P(('shard', 'context'), 'tensor'), may hold values from -0.1875 to 0.1875
- value_weight: bfloat16 [1024, 512], P(('shard', 'context'), 'tensor'), may hold values from -0.1875 to 0.1875
- query_gain: float32 [64], replicated, may hold values from 0.25 to 1.75
- key_gain: float32 [64], replicated, may hold values from 0.25 to 1.75
- output_weight: bfloat16 [1024, 1024], P(('shard', 'context'), 'tensor'), may hold values from -0.75 to 0.75
- feedforward_gain: float32 [1024], replicated, may hold values from 0.25 to 1.75
- gate_weight: bfloat16 [1024, 4608], P(('shard', 'context'), 'tensor'), may hold values from -0.1875 to 0.1875
- up_weight: bfloat16 [1024, 4608], P(('shard', 'context'), 'tensor'), may hold values from -0.1875 to 0.1875
- down_weight: bfloat16 [1024, 4608], P(('shard', 'context'), 'tensor'), may hold values from -0.125 to 0.125
- cotangent: bfloat16 [16384, 1024], P(('shard', 'context', 'tensor')), may hold values from -6 to 6
Outputs:
- block_output: float32 [16384, 1024], P(('shard', 'context', 'tensor'))
- token_grad: float32 [16384, 1024], P(('shard', 'context', 'tensor'))
- attention_gain_grad: float32 [1024], replicated
- query_weight_grad: float32 [1024, 1024], P(('shard', 'context'), 'tensor')
- key_weight_grad: float32 [1024, 512], P(('shard', 'context'), 'tensor')
- value_weight_grad: float32 [1024, 512], P(('shard', 'context'), 'tensor')
- query_gain_grad: float32 [64], replicated
- key_gain_grad: float32 [64], replicated
- output_weight_grad: float32 [1024, 1024], P(('shard', 'context'), 'tensor')
- feedforward_gain_grad: float32 [1024], replicated
- gate_weight_grad: float32 [1024, 4608], P(('shard', 'context'), 'tensor')
- up_weight_grad: float32 [1024, 4608], P(('shard', 'context'), 'tensor')
- down_weight_grad: float32 [1024, 4608], P(('shard', 'context'), 'tensor')
The draws below stay inside these ranges and needn't reach their ends.
Inputs may be any that keep to these rules, and one draw needn't show every extreme that they name: `segments`: in each group's row the document numbers start at 0, never fall and rise by at most one from one token to the next; every group holds the same number of documents; each document holds 1 to 1024 tokens, and exactly one document of each group holds 1024.
All inputs are finite; a program needn't handle non-finite values.
Results may differ from the reference program's by a relative error of at most 0.017.
Values may be sent and summed in bfloat16 or wider, within the bound.
A program may use at most 192 MiB of HBM per device.

```python
import jax
import jax.numpy as jnp
from jax import lax

D = 1024
QHEADS = 16
KVHEADS = 8
HEAD = 64
FF = 4608
TOK_DEV = 512
BLK = 128
MAXLEN = 1024
GROUP_TOK = 2048
GROUPS = 8
TOKENS = 16384
N_SHARD = 2
N_CONTEXT = 4
N_TENSOR = 4


def draw_segments(key, part):
    key = jax.random.fold_in(key, 7)
    begin_key, order_key = jax.random.split(key)
    half_len = MAXLEN // 2
    rest_len = GROUP_TOK - MAXLEN
    if rest_len == 0:
        return jnp.zeros((GROUPS, GROUP_TOK), dtype=jnp.int32)
    extra_cuts = rest_len // half_len
    places = jnp.arange(GROUP_TOK, dtype=jnp.int32)[None, :]
    begin = half_len * jax.random.randint(begin_key, (GROUPS, 1), 0, rest_len // half_len + 1)
    inside = (places >= begin) & (places < begin + MAXLEN)
    rest_place = jnp.where(places < begin, places, places - MAXLEN)
    group_keys = jax.random.split(order_key, GROUPS)
    ranks = jax.vmap(lambda one_key: jax.random.permutation(one_key, rest_len))(group_keys).astype(jnp.int32)
    candidate = jnp.arange(rest_len, dtype=jnp.int32) % half_len != 0
    scored = jnp.where(candidate[None, :], ranks, rest_len)
    cutoff = jnp.sort(scored, axis=1)[:, extra_cuts - 1:extra_cuts]
    chosen = candidate[None, :] & (scored <= cutoff)
    lookup = jnp.clip(rest_place, 0, rest_len - 1)
    chosen_here = jnp.take_along_axis(chosen, jnp.broadcast_to(lookup, (GROUPS, GROUP_TOK)), axis=1)
    starts = jnp.where(inside, places == begin, (rest_place % half_len == 0) | chosen_here)
    return jnp.cumsum(starts.astype(jnp.int32), axis=1) - 1


def levels(rng, dims, pieces, smallest, top_value):
    def one(dim, shards_of):
        heights = jax.random.uniform(jax.random.fold_in(jax.random.fold_in(rng, 6), dim), (shards_of,), jnp.float32, smallest / len(pieces), top_value / len(pieces))
        return jnp.repeat(jnp.exp(heights), dims[dim] // shards_of).reshape((-1,) + (1,) * (len(dims) - dim - 1))

    level = one(*pieces[0])
    for cut in pieces[1:]:
        level = level * one(*cut)
    return level


def centred(stream_key, dims, scale, reach, shards=(), kind=jnp.bfloat16):
    drawn = jax.random.normal(stream_key, dims, jnp.float32) * scale
    if len(shards) > 0:
        drawn = levels(stream_key, dims, shards, -0.22, 0.18) * drawn
    return jnp.clip(drawn, min=-reach, max=reach).astype(kind)


def setup_inputs(seed: int = 0) -> dict:
    streams_of = jax.random.split(jax.random.key(seed), 15)
    tokens = centred(streams_of[0], (TOKENS, D), 1.0, 6.0, ((0, 32),))
    segments = draw_segments(jax.random.fold_in(streams_of[14], 71), 0)
    attention_gain = jnp.clip(1.0 + 0.15 * jax.random.normal(streams_of[2], (D,), jnp.float32), 0.25, 1.75)
    query_weight = centred(streams_of[3], (D, QHEADS * HEAD), D ** -0.5, 0.1875, ((0, 8), (1, 4)))
    key_weight = centred(streams_of[4], (D, KVHEADS * HEAD), D ** -0.5, 0.1875, ((0, 8), (1, 4)))
    value_weight = centred(streams_of[5], (D, KVHEADS * HEAD), D ** -0.5, 0.1875, ((0, 8), (1, 4)))
    query_gain = jnp.clip(1.0 + 0.15 * jax.random.normal(streams_of[6], (HEAD,), jnp.float32), 0.25, 1.75)
    key_gain = jnp.clip(1.0 + 0.15 * jax.random.normal(streams_of[7], (HEAD,), jnp.float32), 0.25, 1.75)
    output_weight = centred(streams_of[8], (D, QHEADS * HEAD), (QHEADS * HEAD // 16) ** -0.5, 0.75, ((0, 8), (1, 4)))
    feedforward_gain = jnp.clip(1.0 + 0.15 * jax.random.normal(streams_of[9], (D,), jnp.float32), 0.25, 1.75)
    gate_weight = centred(streams_of[10], (D, FF), D ** -0.5, 0.1875, ((0, 8), (1, 4)))
    up_weight = centred(streams_of[11], (D, FF), D ** -0.5, 0.1875, ((0, 8), (1, 4)))
    down_weight = centred(streams_of[12], (D, FF), (FF // 2) ** -0.5, 0.125, ((0, 8), (1, 4)))
    cotangent = centred(streams_of[13], (TOKENS, D), 1.0, 6.0, ((0, 32),))
    return dict(tokens=tokens, segments=segments, attention_gain=attention_gain, query_weight=query_weight, key_weight=key_weight, value_weight=value_weight, query_gain=query_gain, key_gain=key_gain, output_weight=output_weight, feedforward_gain=feedforward_gain, gate_weight=gate_weight, up_weight=up_weight, down_weight=down_weight, cotangent=cotangent)


epsilon = 1e-05
rope_base = 1000000.0
top_precision = lax.Precision.HIGHEST

@jax.custom_vjp
def low(v):
    return lax.optimization_barrier(v.astype(jnp.bfloat16)).astype(jnp.float32)

@jax.custom_vjp
def low_back(v):
    return v

def low_keep(v):
    return (low(v), None)

def low_pass(kept, grad):
    return (grad,)

def back_keep(v):
    return (v, None)

def back_low(kept, grad):
    return (low(grad),)
low.defvjp(low_keep, low_pass)
low_back.defvjp(back_keep, back_low)

def matmul(left, right):
    return jnp.dot(left, right, precision=top_precision, preferred_element_type=jnp.float32)

def times_transposed(left, right):
    return lax.dot_general(left, right, (((1,), (1,)), ((), ())), precision=top_precision, preferred_element_type=jnp.float32)

def rms_norm(values, gain_vec):
    return values * lax.rsqrt(lax.optimization_barrier(jnp.mean(values * values, axis=-1, keepdims=True)) + epsilon) * gain_vec

def rotate(values, cosine, sine_table):
    half_dim = values.shape[-1] // 2
    turned = jnp.concatenate([-values[..., half_dim:], values[..., :half_dim]], axis=-1)
    return values * cosine + turned * sine_table

def tables(segment_row):
    length = segment_row.shape[0]
    places = jnp.arange(length, dtype=jnp.int32)
    seg_start = jnp.concatenate([jnp.ones((1,), dtype=jnp.bool_), segment_row[1:] != segment_row[:-1]])
    starts = lax.cummax(jnp.where(seg_start, places, jnp.zeros_like(places)), axis=0)
    position = (places - starts).astype(jnp.float32)
    frequency = rope_base ** (-2.0 * jnp.arange(HEAD // 2, dtype=jnp.float32) / HEAD)
    angles = position[:, None] * frequency[None, :]
    angles = jnp.concatenate([angles, angles], axis=1)
    return (position, jnp.cos(angles), jnp.sin(angles))

def attend(query_rot, key_rot, value_heads, segment_row, position):
    block_rows = min(512, GROUP_TOK)
    block_count = GROUP_TOK // block_rows
    score_scale = HEAD ** (-0.5)

    def one_block(inputs):
        query_block, seg_block, pos_block = inputs
        grouped = query_block.reshape(block_rows, KVHEADS, QHEADS // KVHEADS, HEAD)
        scores = jnp.einsum('bgrh,kgh->grbk', grouped, key_rot, precision=top_precision, preferred_element_type=jnp.float32) * score_scale
        allowed = (seg_block[:, None] == segment_row[None, :]) & (position[None, :] <= pos_block[:, None])
        scores = low_back(jnp.where(allowed[None, None], scores, -1e+30))
        row_max = lax.optimization_barrier(jnp.max(scores, axis=-1, keepdims=True))
        lifted = jnp.exp(scores - row_max)
        weights = low(lifted / lax.optimization_barrier(jnp.sum(lifted, axis=-1, keepdims=True)))
        mixture = jnp.einsum('grbk,kgh->bgrh', weights, value_heads, precision=top_precision, preferred_element_type=jnp.float32)
        return mixture.reshape(block_rows, QHEADS * HEAD)
    combined = lax.map(jax.checkpoint(one_block), (query_rot.reshape(block_count, block_rows, QHEADS, HEAD), segment_row.reshape(block_count, block_rows), position.reshape(block_count, block_rows)))
    return combined.reshape(GROUP_TOK, QHEADS * HEAD)

def group_forward(stream_rows, segment_row, attention_gain, query_weight, key_weight, value_weight, query_gain, key_gain, output_weight, feedforward_gain, gate_weight, up_weight, down_weight):
    position, cosine, sine_table = tables(segment_row)
    normed_in = low(rms_norm(stream_rows, attention_gain))
    query_raw = low(low_back(matmul(normed_in, query_weight))).reshape(GROUP_TOK, QHEADS, HEAD)
    key_raw = low(low_back(matmul(normed_in, key_weight))).reshape(GROUP_TOK, KVHEADS, HEAD)
    value_raw = low(low_back(matmul(normed_in, value_weight))).reshape(GROUP_TOK, KVHEADS, HEAD)
    query_rot = low(rotate(rms_norm(query_raw, query_gain), cosine[:, None, :], sine_table[:, None, :]))
    key_rot = low(rotate(rms_norm(key_raw, key_gain), cosine[:, None, :], sine_table[:, None, :]))
    attended = low(low_back(attend(query_rot, key_rot, value_raw, segment_row, position)))
    hidden_in = stream_rows + low_back(times_transposed(attended, output_weight))
    normed_mid = low(rms_norm(hidden_in, feedforward_gain))
    gate_pre = low_back(matmul(normed_mid, gate_weight))
    up_pre = low_back(matmul(normed_mid, up_weight))
    activated = low(gate_pre * jax.nn.sigmoid(gate_pre) * up_pre)
    return hidden_in + times_transposed(activated, down_weight)

def reference(tokens, segments, attention_gain, query_weight, key_weight, value_weight, query_gain, key_gain, output_weight, feedforward_gain, gate_weight, up_weight, down_weight, cotangent):
    block_count = TOK_DEV // BLK

    def arrange(values):
        shaped = values.astype(jnp.float32).reshape(N_SHARD, N_CONTEXT, N_TENSOR, block_count, BLK, D)
        return shaped.transpose(0, 2, 3, 1, 4, 5).reshape(GROUPS, GROUP_TOK, D)

    def restore(values):
        shaped = values.reshape(N_SHARD, N_TENSOR, block_count, N_CONTEXT, BLK, D)
        return shaped.transpose(0, 3, 1, 2, 4, 5).reshape(TOKENS, D)
    params = tuple((item.astype(jnp.float32) for item in (attention_gain, query_weight, key_weight, value_weight, query_gain, key_gain, output_weight, feedforward_gain, gate_weight, up_weight, down_weight)))

    def forward(stream, *weights):

        def advance(carried, inputs):
            return (carried, jax.checkpoint(group_forward)(inputs[0], inputs[1], *weights))
        _, outputs = lax.scan(advance, None, (stream, segments))
        return outputs
    outputs, pullback = jax.vjp(forward, arrange(tokens), *params)
    gradients = pullback(arrange(cotangent))
    return (restore(outputs), restore(gradients[0]), gradients[1], gradients[2], gradients[3], gradients[4], gradients[5], gradients[6], gradients[7], gradients[8], gradients[9], gradients[10], gradients[11])
```

```python
import jax
import jax.numpy as jnp
from jax import lax
from jax.experimental import pallas as pl
from jax.experimental.pallas import tpu as pltpu
from jax.sharding import PartitionSpec as P

QHEADS = 16
KVHEADS = 8
HEAD = 64
BLK = 128
MAXLEN = 1024
PAIR = 2 * HEAD


epsilon = 1e-05
rope_base = 1000000.0
contract_rows = (((0,), (0,)), ((), ()))
contract_cols = (((1,), (1,)), ((), ()))


def rms_norm(values, gain_vec):
    return (
        values * lax.rsqrt(jnp.mean(values * values, axis=-1, keepdims=True) + epsilon) * gain_vec
    )


def tables(segment_row):
    length = segment_row.shape[0]
    places = jnp.arange(length, dtype=jnp.int32)
    seg_start = jnp.concatenate(
        [jnp.ones((1,), dtype=jnp.bool_), segment_row[1:] != segment_row[:-1]]
    )
    starts = lax.cummax(jnp.where(seg_start, places, jnp.zeros_like(places)), axis=0)
    position = (places - starts).astype(jnp.float32)
    frequency = rope_base ** (-2.0 * jnp.arange(HEAD // 2, dtype=jnp.float32) / HEAD)
    angles = position[:, None] * frequency[None, :]
    cosine, sine = jnp.cos(angles), jnp.sin(angles)
    wide = PAIR // (HEAD // 2)
    return (
        starts[:, None],
        jnp.concatenate([cosine] * wide, axis=1),
        jnp.concatenate([sine] * wide, axis=1),
    )


def product(left, right):
    return jnp.dot(left, right, preferred_element_type=jnp.float32)


def product_cols(left, right):
    return lax.dot_general(left, right, contract_cols, preferred_element_type=jnp.float32)


def product_rows(left, right):
    return lax.dot_general(left, right, contract_rows, preferred_element_type=jnp.float32)


def silu_parts(gate_pre):
    logistic = jax.nn.sigmoid(gate_pre)
    return (gate_pre * logistic, logistic * (1.0 + gate_pre * (1.0 - logistic)))


def lane_half(rows):
    return lax.broadcasted_iota(jnp.int32, (rows, PAIR), 1) // HEAD


def half_mean(values, half):
    low_sum = jnp.sum(jnp.where(half == 0, values, 0.0), axis=1, keepdims=True)
    high_sum = jnp.sum(jnp.where(half == 0, 0.0, values), axis=1, keepdims=True)
    return jnp.where(half == 0, low_sum, high_sum) * (1.0 / HEAD)


def first_quarter(rows):
    lanes = lax.broadcasted_iota(jnp.int32, (rows, PAIR), 1)
    return lanes % HEAD < HEAD // 2


def norm_rope(values, gain, cosine, sine):
    rows = values.shape[0]
    inverse = lax.rsqrt(half_mean(values * values, lane_half(rows)) + epsilon)
    normed = values * inverse * gain
    turned = jnp.where(
        first_quarter(rows),
        -pltpu.roll(normed, PAIR - HEAD // 2, 1),
        pltpu.roll(normed, HEAD // 2, 1),
    )
    return normed * cosine + turned * sine


def norm_rope_back(grad, values, gain, cosine, sine):
    rows = values.shape[0]
    half = lane_half(rows)
    inverse = lax.rsqrt(half_mean(values * values, half) + epsilon)
    turned = jnp.where(
        first_quarter(rows),
        pltpu.roll(grad * sine, PAIR - HEAD // 2, 1),
        -pltpu.roll(grad * sine, HEAD // 2, 1),
    )
    d_normed = grad * cosine + turned
    gain_grad = jnp.sum(d_normed * values * inverse, axis=0, keepdims=True)
    scaled = d_normed * gain
    d_values = inverse * scaled - values * (inverse * inverse * inverse) * half_mean(
        scaled * values, half
    )
    return d_values, gain_grad


def twice(values, which):
    return jnp.where(lane_half(values.shape[0]) == which, values, pltpu.roll(values, HEAD, 1))


def stacked(values):
    half = lane_half(values.shape[0])
    return jnp.concatenate(
        [jnp.where(half == 0, values, 0.0), jnp.where(half == 0, 0.0, values)], axis=0
    ).astype(jnp.bfloat16)


def unstacked(values):
    half = lane_half(BLK)
    return jnp.where(half == 0, values[:BLK], values[BLK:])


def arrival(stream_block, contexts, blocks):
    return (stream_block % contexts) * blocks + stream_block // contexts


def prepare_keys(dims, k_ref, v_ref, cos_ref, sin_ref, kgain_ref, keys, values):
    contexts, blocks, _ = dims
    which = pl.program_id(0)

    @pl.when(pl.program_id(1) == 0)
    def _():
        def one(block, carried):
            source = pl.ds(pl.multiple_of(arrival(block, contexts, blocks) * BLK, BLK), BLK)
            target = pl.ds(pl.multiple_of(block * BLK, BLK), BLK)
            raw = twice(k_ref[source, :].astype(jnp.float32), which)
            keys[target, :] = norm_rope(
                raw, kgain_ref[...], cos_ref[target, :], sin_ref[target, :]
            ).astype(jnp.bfloat16)
            values[target, :] = twice(v_ref[source, :].astype(jnp.float32), which).astype(
                jnp.bfloat16
            )
            return carried

        lax.fori_loop(0, contexts * blocks, one, 0)


def block_probs(dims, q_ref, cos_ref, sin_ref, start_ref, qgain_ref, keys):
    window = dims[2]
    block = pl.program_id(1)
    here = pl.ds(pl.multiple_of(block * BLK, BLK), BLK)
    query_raw = q_ref[...].astype(jnp.float32)
    query = stacked(norm_rope(query_raw, qgain_ref[...], cos_ref[here, :], sin_ref[here, :]))
    first = pl.multiple_of(jnp.maximum(block * BLK + BLK - window, 0), BLK)
    span = pl.ds(first, window)
    scores = product_cols(query, keys[span, :]) * (HEAD ** (-0.5))
    shape = (BLK, window)
    column = lax.broadcasted_iota(jnp.int32, shape, 1) + first
    row = lax.broadcasted_iota(jnp.int32, shape, 0) + block * BLK
    allowed = (column >= start_ref[here, :]) & (column <= row)
    offset = jnp.where(allowed, 0.0, -1e30)
    scores = scores + jnp.concatenate([offset, offset], axis=0)
    lifted = jnp.exp(scores - jnp.max(scores, axis=1, keepdims=True))
    probs = lifted * (1.0 / jnp.sum(lifted, axis=1, keepdims=True))
    return query_raw, query, span, here, probs


def forward_kernel(
    dims, q_ref, k_ref, v_ref, cos_ref, sin_ref, start_ref, qgain_ref, kgain_ref, o_ref, keys, values
):
    prepare_keys(dims, k_ref, v_ref, cos_ref, sin_ref, kgain_ref, keys, values)
    _, _, span, _, probs = block_probs(
        dims, q_ref, cos_ref, sin_ref, start_ref, qgain_ref, keys
    )
    mixture = product(probs.astype(jnp.bfloat16), values[span, :])
    o_ref[...] = unstacked(mixture).astype(o_ref.dtype)


def backward_kernel(
    dims,
    q_ref,
    k_ref,
    v_ref,
    cos_ref,
    sin_ref,
    start_ref,
    qgain_ref,
    kgain_ref,
    d_ref,
    dq_ref,
    dk_ref,
    dv_ref,
    dqgain_ref,
    dkgain_ref,
    keys,
    values,
    key_acc,
    value_acc,
):
    contexts, blocks, _ = dims
    which = pl.program_id(0)
    block = pl.program_id(1)
    scale = HEAD ** (-0.5)
    prepare_keys(dims, k_ref, v_ref, cos_ref, sin_ref, kgain_ref, keys, values)

    @pl.when(block == 0)
    def _():
        key_acc[...] = jnp.zeros_like(key_acc)
        value_acc[...] = jnp.zeros_like(value_acc)

    @pl.when((block == 0) & (which == 0))
    def _():
        dqgain_ref[...] = jnp.zeros_like(dqgain_ref)
        dkgain_ref[...] = jnp.zeros_like(dkgain_ref)

    query_raw, query, span, here, probs = block_probs(
        dims, q_ref, cos_ref, sin_ref, start_ref, qgain_ref, keys
    )
    grad = stacked(d_ref[...].astype(jnp.float32))
    d_probs = product_cols(grad, values[span, :])
    row_dot = jnp.sum(probs * d_probs, axis=1, keepdims=True)
    d_scores = (probs * (d_probs - row_dot)).astype(jnp.bfloat16)
    value_acc[span, :] += product_rows(probs.astype(jnp.bfloat16), grad)
    key_acc[span, :] += product_rows(d_scores, query)
    d_query_rot = unstacked(product(d_scores, keys[span, :])) * scale
    d_query, gain_grad = norm_rope_back(
        d_query_rot, query_raw, qgain_ref[...], cos_ref[here, :], sin_ref[here, :]
    )
    dq_ref[...] = d_query.astype(dq_ref.dtype)
    dqgain_ref[0:1, :] += gain_grad

    @pl.when(block == contexts * blocks - 1)
    def _():
        half = lane_half(BLK)

        def one(item, carried):
            place = pl.ds(pl.multiple_of(arrival(item, contexts, blocks) * BLK, BLK), BLK)
            stream = pl.ds(pl.multiple_of(item * BLK, BLK), BLK)
            raw = twice(k_ref[place, :].astype(jnp.float32), which)
            d_key_rot = key_acc[stream, :]
            d_key_rot = (d_key_rot + pltpu.roll(d_key_rot, HEAD, 1)) * scale
            d_key, key_gain_grad = norm_rope_back(
                d_key_rot, raw, kgain_ref[...], cos_ref[stream, :], sin_ref[stream, :]
            )
            dkgain_ref[0:1, :] += key_gain_grad
            d_value = value_acc[stream, :]
            d_value = d_value + pltpu.roll(d_value, HEAD, 1)
            old_key = dk_ref[place, :].astype(jnp.float32)
            old_value = dv_ref[place, :].astype(jnp.float32)
            mine = half == which
            later = which > 0
            old_key = jnp.where(later, old_key, 0.0)
            old_value = jnp.where(later, old_value, 0.0)
            dk_ref[place, :] = jnp.where(mine, d_key, old_key).astype(dk_ref.dtype)
            dv_ref[place, :] = jnp.where(mine, d_value, old_value).astype(dv_ref.dtype)
            return carried

        lax.fori_loop(0, contexts * blocks, one, 0)


def attention(backward, contexts, qkv, cosine, sine, starts, gain_query, gain_key, d_attended):
    rows = qkv.shape[0]
    stream_blocks = rows // BLK
    blocks = stream_blocks // contexts
    window = min(MAXLEN + BLK, rows)
    pairs = QHEADS // contexts // 2
    dims = (contexts, blocks, window)

    def moving():
        return pl.BlockSpec((BLK, PAIR), lambda g, s: (arrival(s, contexts, blocks), g))

    def whole(shape, column=0):
        return pl.BlockSpec(shape, lambda g, s: (0, column))

    tall = (rows, PAIR)
    in_specs = [
        moving(),
        whole(tall, pairs),
        whole(tall, pairs + 1),
        whole(tall),
        whole(tall),
        whole((rows, 1)),
        whole((1, PAIR)),
        whole((1, PAIR)),
    ]
    operands = [
        qkv,
        qkv,
        qkv,
        cosine,
        sine,
        starts,
        jnp.concatenate([gain_query, gain_query])[None, :],
        jnp.concatenate([gain_key, gain_key])[None, :],
    ]
    scratch = [pltpu.VMEM(tall, jnp.bfloat16), pltpu.VMEM(tall, jnp.bfloat16)]
    params = pltpu.CompilerParams(
        dimension_semantics=("arbitrary", "arbitrary"), vmem_limit_bytes=48 * 1024 * 1024
    )
    products = 2 * 2 * stream_blocks * BLK * window * PAIR * pairs
    if not backward:
        return pl.pallas_call(
            lambda *refs: forward_kernel(dims, *refs),
            grid=(pairs, stream_blocks),
            in_specs=in_specs,
            out_specs=moving(),
            out_shape=jax.ShapeDtypeStruct((rows, pairs * PAIR), jnp.bfloat16),
            scratch_shapes=scratch,
            compiler_params=params,
            cost_estimate=pl.CostEstimate(
                flops=2 * products, bytes_accessed=10 * rows * PAIR * 4, transcendentals=0
            ),
            name="attention_forward",
        )(*operands)
    accs = [pltpu.VMEM(tall, jnp.float32), pltpu.VMEM(tall, jnp.float32)]
    return pl.pallas_call(
        lambda *refs: backward_kernel(dims, *refs),
        grid=(pairs, stream_blocks),
        in_specs=in_specs + [moving()],
        out_specs=[moving(), whole(tall), whole(tall), whole((8, PAIR)), whole((8, PAIR))],
        out_shape=[
            jax.ShapeDtypeStruct((rows, pairs * PAIR), jnp.bfloat16),
            jax.ShapeDtypeStruct(tall, jnp.bfloat16),
            jax.ShapeDtypeStruct(tall, jnp.bfloat16),
            jax.ShapeDtypeStruct((8, PAIR), jnp.float32),
            jax.ShapeDtypeStruct((8, PAIR), jnp.float32),
        ],
        scratch_shapes=scratch + accs,
        compiler_params=params,
        cost_estimate=pl.CostEstimate(
            flops=5 * products, bytes_accessed=16 * rows * PAIR * 4, transcendentals=0
        ),
        name="attention_backward",
    )(*operands, d_attended)


def on_device(
    tokens,
    segments,
    attention_gain,
    query_weight,
    key_weight,
    value_weight,
    query_gain,
    key_gain,
    output_weight,
    feedforward_gain,
    gate_weight,
    up_weight,
    down_weight,
    cotangent,
):
    contexts = lax.axis_size("context")
    tensors = lax.axis_size("tensor")
    tok_rows = tokens.shape[0]
    group_rows = segments.shape[1]
    hidden = gate_weight.shape[1]
    width = tokens.shape[1]
    query_cols = query_weight.shape[1]
    kv_cols = key_weight.shape[1]
    qkv_cols = query_cols + 2 * kv_cols
    rows_axes = ("shard", "context")
    bfloat = jnp.bfloat16

    def shift(values, step):
        pairs = [(i, (i + step) % tensors) for i in range(tensors)]
        return lax.ppermute(values, "tensor", pairs)

    attn_local = jnp.concatenate([query_weight, key_weight, value_weight, output_weight], axis=1)
    attn_cols = lax.all_gather(attn_local, "tensor", axis=0)
    qkv_weight = lax.all_gather(attn_cols[:, :, :qkv_cols], rows_axes, axis=1, tiled=True)
    grad_rows = [cotangent] + [shift(cotangent, step) for step in range(1, tensors)]

    starts, cosine, sine = tables(segments[0])
    inputs_f32 = tokens.astype(jnp.float32)
    normed_f32, norm_in_pull = jax.vjp(rms_norm, inputs_f32, attention_gain)
    normed_in = normed_f32.astype(bfloat)

    qkv_weight, out_local, gate_local, up_local, down_local = lax.optimization_barrier(
        (qkv_weight, attn_cols[:, :, qkv_cols:], gate_weight, up_weight, down_weight)
    )
    out_weight = lax.all_gather(out_local, rows_axes, axis=1, tiled=True)
    pair_weight = lax.all_gather(
        jnp.concatenate([gate_local, up_local], axis=1), rows_axes, axis=0, tiled=True
    )
    down_full = lax.all_gather(down_local, rows_axes, axis=0, tiled=True)

    qkv_send = jnp.einsum(
        "md,tdn->tmn", normed_in, qkv_weight, preferred_element_type=jnp.float32
    ).astype(bfloat)
    qkv = lax.all_to_all(qkv_send, "context", split_axis=0, concat_axis=0, tiled=True)
    qkv = qkv.reshape(group_rows, qkv_cols)
    mixed = attention(
        False, contexts, qkv, cosine, sine, starts, query_gain, key_gain, None
    )
    attended = lax.all_to_all(
        mixed.reshape(contexts, tok_rows, query_cols),
        "context",
        split_axis=0,
        concat_axis=0,
        tiled=True,
    )
    hidden_in = inputs_f32 + jnp.einsum(
        "tmk,tdk->md", attended, out_weight, preferred_element_type=jnp.float32
    )
    mid_f32, mid_pull = jax.vjp(rms_norm, hidden_in, feedforward_gain)
    normed_mid = mid_f32.astype(bfloat)
    normed_rows = [normed_mid] + [shift(normed_mid, step) for step in range(1, tensors)]

    outputs_part, grads_part = [], []
    pair_grad = down_grad = None
    for step in range(tensors):
        pre = product(normed_rows[step], pair_weight)
        d_activated = product(grad_rows[step], down_full)
        gate_pre, up_pre = pre[:, :hidden], pre[:, hidden:]
        silu_gate, silu_slope = silu_parts(gate_pre)
        activated = (silu_gate * up_pre).astype(bfloat)
        d_gate = (d_activated * up_pre * silu_slope).astype(bfloat)
        d_up = (d_activated * silu_gate).astype(bfloat)
        d_pair = jnp.concatenate([d_gate, d_up], axis=1)
        d_mid = product_cols(d_pair, pair_weight)
        if step > 0:
            d_mid = shift(d_mid.astype(bfloat), -step).astype(jnp.float32)
        grads_part.append(d_mid)
        outputs_part.append(product_cols(activated, down_full))
        pair_term = product_rows(normed_rows[step], d_pair)
        down_term = product_rows(grad_rows[step], activated)
        pair_grad = pair_term if step == 0 else pair_grad + pair_term
        down_grad = down_term if step == 0 else down_grad + down_term
    pair_owned = lax.psum_scatter(
        pair_grad.astype(bfloat), rows_axes, scatter_dimension=0, tiled=True
    )
    down_owned = lax.psum_scatter(
        down_grad.astype(bfloat), rows_axes, scatter_dimension=0, tiled=True
    )
    d_normed_mid = sum(grads_part[1:], grads_part[0])
    d_normed_mid, *late = lax.optimization_barrier(
        (d_normed_mid, *[part.astype(bfloat) for part in outputs_part[1:]])
    )
    ffn_output = outputs_part[0]
    for step in range(1, tensors):
        ffn_output = ffn_output + shift(late[step - 1], -step).astype(jnp.float32)
    block_output = hidden_in + ffn_output

    d_hidden_mid, feedforward_gain_grad = mid_pull(d_normed_mid)
    d_hidden = cotangent.astype(jnp.float32) + d_hidden_mid
    d_branch = d_hidden.astype(bfloat)
    d_attended_send = jnp.einsum(
        "md,tdk->tmk", d_branch, out_weight, preferred_element_type=jnp.float32
    ).astype(bfloat)
    d_attended = lax.all_to_all(
        d_attended_send, "context", split_axis=0, concat_axis=0, tiled=True
    ).reshape(group_rows, query_cols)
    out_grad = jnp.einsum(
        "md,tmk->tdk", d_branch, attended, preferred_element_type=jnp.float32
    ).astype(bfloat)
    out_rows = lax.psum_scatter(out_grad, rows_axes, scatter_dimension=1, tiled=True)

    d_query_here, d_key_here, d_value_here, query_gain_rows, key_gain_rows = attention(
        True, contexts, qkv, cosine, sine, starts, query_gain, key_gain, d_attended
    )
    query_gain_grad = query_gain_rows[0, :HEAD] + query_gain_rows[0, HEAD:]
    key_gain_grad = key_gain_rows[0, :HEAD]
    d_qkv_send = jnp.concatenate([d_query_here, d_key_here, d_value_here], axis=1)
    d_qkv = lax.all_to_all(
        d_qkv_send.reshape(contexts, tok_rows, qkv_cols),
        "context",
        split_axis=0,
        concat_axis=0,
        tiled=True,
    )
    qkv_grad = jnp.einsum(
        "md,tmn->tdn", normed_in, d_qkv, preferred_element_type=jnp.float32
    ).astype(bfloat)
    qkv_grad, pair_owned, down_owned, out_rows = lax.optimization_barrier(
        (qkv_grad, pair_owned, down_owned, out_rows)
    )
    qkv_rows = lax.psum_scatter(qkv_grad, rows_axes, scatter_dimension=1, tiled=True)
    d_normed_in = jnp.einsum(
        "tmn,tdn->md", d_qkv, qkv_weight, preferred_element_type=jnp.float32
    )
    d_inputs_norm, attention_gain_grad = norm_in_pull(d_normed_in)
    token_grad = d_hidden + d_inputs_norm
    attn_owned = lax.psum_scatter(
        jnp.concatenate([qkv_rows, out_rows], axis=2), "tensor", scatter_dimension=0, tiled=True
    )[0].astype(jnp.float32)
    gains = jnp.concatenate(
        [attention_gain_grad, feedforward_gain_grad, query_gain_grad, key_gain_grad]
    )
    gains = lax.all_gather(gains[None, :], ("shard", "context", "tensor"), axis=0, tiled=True)
    gains = jnp.sum(gains, axis=0)
    pair_owned = pair_owned.astype(jnp.float32)
    return (
        block_output,
        token_grad,
        gains[:width],
        attn_owned[:, :query_cols],
        attn_owned[:, query_cols : query_cols + kv_cols],
        attn_owned[:, query_cols + kv_cols : qkv_cols],
        gains[2 * width : 2 * width + HEAD],
        gains[2 * width + HEAD :],
        attn_owned[:, qkv_cols:],
        gains[width : 2 * width],
        pair_owned[:, :hidden],
        pair_owned[:, hidden:],
        down_owned.astype(jnp.float32),
    )


def solution(mesh):
    placed = (
        P(("shard", "context", "tensor"), None),
        P(("shard", "tensor"), None),
        P(),
        P(("shard", "context"), "tensor"),
        P(("shard", "context"), "tensor"),
        P(("shard", "context"), "tensor"),
        P(),
        P(),
        P(("shard", "context"), "tensor"),
        P(),
        P(("shard", "context"), "tensor"),
        P(("shard", "context"), "tensor"),
        P(("shard", "context"), "tensor"),
        P(("shard", "context", "tensor"), None),
    )
    return jax.shard_map(
        on_device,
        mesh=mesh,
        in_specs=placed,
        out_specs=(
            P(("shard", "context", "tensor"), None),
            P(("shard", "context", "tensor"), None),
            P(),
            P(("shard", "context"), "tensor"),
            P(("shard", "context"), "tensor"),
            P(("shard", "context"), "tensor"),
            P(),
            P(),
            P(("shard", "context"), "tensor"),
            P(),
            P(("shard", "context"), "tensor"),
            P(("shard", "context"), "tensor"),
            P(("shard", "context"), "tensor"),
        ),
        check_vma=False,
    )
```

```python
import jax
import jax.numpy as jnp
from jax import lax
from jax.experimental import pallas as pl
from jax.experimental.pallas import tpu as pltpu
from jax.sharding import PartitionSpec as P

QHEADS = 16
KVHEADS = 8
HEAD = 64
BLK = 128
MAXLEN = 1024
PAIR = 2 * HEAD


epsilon = 1e-05
rope_base = 1000000.0
contract_rows = (((0,), (0,)), ((), ()))
contract_cols = (((1,), (1,)), ((), ()))


def rms_norm(values, gain_vec):
    return (
        values * lax.rsqrt(jnp.mean(values * values, axis=-1, keepdims=True) + epsilon) * gain_vec
    )


def tables(segment_row):
    length = segment_row.shape[0]
    places = jnp.arange(length, dtype=jnp.int32)
    seg_start = jnp.concatenate(
        [jnp.ones((1,), dtype=jnp.bool_), segment_row[1:] != segment_row[:-1]]
    )
    starts = lax.cummax(jnp.where(seg_start, places, jnp.zeros_like(places)), axis=0)
    position = (places - starts).astype(jnp.float32)
    frequency = rope_base ** (-2.0 * jnp.arange(HEAD // 2, dtype=jnp.float32) / HEAD)
    angles = position[:, None] * frequency[None, :]
    cosine, sine = jnp.cos(angles), jnp.sin(angles)
    wide = PAIR // (HEAD // 2)
    return (
        starts.reshape(-1, BLK),
        jnp.concatenate([cosine] * wide, axis=1),
        jnp.concatenate([sine] * wide, axis=1),
    )


def product(left, right):
    return jnp.dot(left, right, preferred_element_type=jnp.float32)


def product_cols(left, right):
    return lax.dot_general(left, right, contract_cols, preferred_element_type=jnp.float32)


def product_rows(left, right):
    return lax.dot_general(left, right, contract_rows, preferred_element_type=jnp.float32)


def silu_parts(gate_pre):
    logistic = jax.nn.sigmoid(gate_pre)
    return (gate_pre * logistic, logistic * (1.0 + gate_pre * (1.0 - logistic)))


def lane_half(rows):
    return lax.broadcasted_iota(jnp.int32, (rows, PAIR), 1) // HEAD


def half_mean(values, half):
    low_sum = jnp.sum(jnp.where(half == 0, values, 0.0), axis=1, keepdims=True)
    high_sum = jnp.sum(jnp.where(half == 0, 0.0, values), axis=1, keepdims=True)
    return jnp.where(half == 0, low_sum, high_sum) * (1.0 / HEAD)


def first_quarter(rows):
    lanes = lax.broadcasted_iota(jnp.int32, (rows, PAIR), 1)
    return lanes % HEAD < HEAD // 2


def norm_rope(values, gain, cosine, sine):
    rows = values.shape[0]
    inverse = lax.rsqrt(half_mean(values * values, lane_half(rows)) + epsilon)
    normed = values * inverse * gain
    turned = jnp.where(
        first_quarter(rows),
        -pltpu.roll(normed, PAIR - HEAD // 2, 1),
        pltpu.roll(normed, HEAD // 2, 1),
    )
    return normed * cosine + turned * sine


def norm_rope_back(grad, values, gain, cosine, sine):
    rows = values.shape[0]
    half = lane_half(rows)
    inverse = lax.rsqrt(half_mean(values * values, half) + epsilon)
    turned = jnp.where(
        first_quarter(rows),
        pltpu.roll(grad * sine, PAIR - HEAD // 2, 1),
        -pltpu.roll(grad * sine, HEAD // 2, 1),
    )
    d_normed = grad * cosine + turned
    gain_grad = jnp.sum(d_normed * values * inverse, axis=0, keepdims=True)
    scaled = d_normed * gain
    d_values = inverse * scaled - values * (inverse * inverse * inverse) * half_mean(
        scaled * values, half
    )
    return d_values, gain_grad


def twice(values, which):
    return jnp.where(lane_half(values.shape[0]) == which, values, pltpu.roll(values, HEAD, 1))


def stacked(values):
    half = lane_half(values.shape[0])
    return jnp.concatenate(
        [jnp.where(half == 0, values, 0.0), jnp.where(half == 0, 0.0, values)], axis=0
    ).astype(jnp.bfloat16)


def unstacked(values):
    half = lane_half(BLK)
    return jnp.where(half == 0, values[:BLK], values[BLK:])


def arrival(stream_block, contexts, blocks):
    return (stream_block % contexts) * blocks + stream_block // contexts


def prepare_keys(dims, k_ref, v_ref, cos_ref, sin_ref, kgain_ref, keys, values):
    contexts, blocks, _ = dims
    which = pl.program_id(0)

    @pl.when(pl.program_id(1) == 0)
    def _():
        def one(block, carried):
            source = pl.ds(pl.multiple_of(arrival(block, contexts, blocks) * BLK, BLK), BLK)
            target = pl.ds(pl.multiple_of(block * BLK, BLK), BLK)
            raw = twice(k_ref[source, :].astype(jnp.float32), which)
            keys[target, :] = norm_rope(
                raw, kgain_ref[...], cos_ref[target, :], sin_ref[target, :]
            ).astype(jnp.bfloat16)
            values[target, :] = twice(v_ref[source, :].astype(jnp.float32), which).astype(
                jnp.bfloat16
            )
            return carried

        lax.fori_loop(0, contexts * blocks, one, 0)


def for_reach(dims, body):
    contexts, blocks, window = dims
    block = pl.program_id(1)
    total = contexts * blocks
    widths = sorted({min(4 * BLK, window), min(8 * BLK, window), window})
    lower = 0
    for width in widths:
        upper = total if width == window else width // BLK

        @pl.when((block >= lower) & (block < upper))
        def _(width=width):
            body(width)

        lower = upper


def block_probs(width, q_ref, cos_ref, sin_ref, start_ref, qgain_ref, keys):
    block = pl.program_id(1)
    here = pl.ds(pl.multiple_of(block * BLK, BLK), BLK)
    query_raw = q_ref[...].astype(jnp.float32)
    query_rot = norm_rope(query_raw, qgain_ref[...], cos_ref[here, :], sin_ref[here, :])
    query = stacked(query_rot.astype(jnp.bfloat16).astype(jnp.float32) * (HEAD ** (-0.5)))
    first = pl.multiple_of(jnp.maximum(block * BLK + BLK - width, 0), BLK)
    span = pl.ds(first, width)
    scores = product_cols(keys[span, :], query)
    shape = (width, BLK)
    key_place = lax.broadcasted_iota(jnp.int32, shape, 0) + first
    query_place = lax.broadcasted_iota(jnp.int32, shape, 1) + block * BLK
    allowed = (key_place >= start_ref[pl.ds(block, 1), :]) & (key_place <= query_place)
    offset = jnp.where(allowed, 0.0, -1e30)
    scores = scores + jnp.concatenate([offset, offset], axis=1)
    lifted = jnp.exp(scores - jnp.max(scores, axis=0, keepdims=True))
    total = jnp.sum(lifted, axis=0, keepdims=True)
    return query_raw, query, span, here, lifted * (1.0 / total)


def forward_kernel(
    dims, q_ref, k_ref, v_ref, cos_ref, sin_ref, start_ref, qgain_ref, kgain_ref, o_ref, keys, values
):
    prepare_keys(dims, k_ref, v_ref, cos_ref, sin_ref, kgain_ref, keys, values)

    def body(width):
        _, _, span, _, probs = block_probs(
            width, q_ref, cos_ref, sin_ref, start_ref, qgain_ref, keys
        )
        mixture = product_rows(values[span, :], probs.astype(jnp.bfloat16))
        o_ref[...] = unstacked(mixture.T).astype(o_ref.dtype)

    for_reach(dims, body)


def backward_kernel(
    dims,
    q_ref,
    k_ref,
    v_ref,
    cos_ref,
    sin_ref,
    start_ref,
    qgain_ref,
    kgain_ref,
    d_ref,
    dq_ref,
    dk_ref,
    dv_ref,
    dqgain_ref,
    dkgain_ref,
    keys,
    values,
    key_acc,
    value_acc,
):
    contexts, blocks, _ = dims
    which = pl.program_id(0)
    block = pl.program_id(1)
    scale = HEAD ** (-0.5)
    prepare_keys(dims, k_ref, v_ref, cos_ref, sin_ref, kgain_ref, keys, values)

    @pl.when(block == 0)
    def _():
        key_acc[...] = jnp.zeros_like(key_acc)
        value_acc[...] = jnp.zeros_like(value_acc)

    @pl.when((block == 0) & (which == 0))
    def _():
        dqgain_ref[...] = jnp.zeros_like(dqgain_ref)
        dkgain_ref[...] = jnp.zeros_like(dkgain_ref)

    def body(width):
        query_raw, query, span, here, probs = block_probs(
            width, q_ref, cos_ref, sin_ref, start_ref, qgain_ref, keys
        )
        grad = stacked(d_ref[...].astype(jnp.float32))
        d_probs = product_cols(values[span, :], grad)
        row_dot = jnp.sum(probs * d_probs, axis=0, keepdims=True)
        d_scores = (probs * (d_probs - row_dot)).astype(jnp.bfloat16)
        value_acc[span, :] += product(probs.astype(jnp.bfloat16), grad)
        key_acc[span, :] += product(d_scores, query)
        d_query_rot = unstacked(product_rows(keys[span, :], d_scores).T) * scale
        d_query, gain_grad = norm_rope_back(
            d_query_rot, query_raw, qgain_ref[...], cos_ref[here, :], sin_ref[here, :]
        )
        dq_ref[...] = d_query.astype(dq_ref.dtype)
        dqgain_ref[0:1, :] += gain_grad

    for_reach(dims, body)

    @pl.when(block == contexts * blocks - 1)
    def _():
        half = lane_half(BLK)

        def one(item, carried):
            place = pl.ds(pl.multiple_of(arrival(item, contexts, blocks) * BLK, BLK), BLK)
            stream = pl.ds(pl.multiple_of(item * BLK, BLK), BLK)
            raw = twice(k_ref[place, :].astype(jnp.float32), which)
            d_key_rot = key_acc[stream, :]
            d_key_rot = d_key_rot + pltpu.roll(d_key_rot, HEAD, 1)
            d_key, key_gain_grad = norm_rope_back(
                d_key_rot, raw, kgain_ref[...], cos_ref[stream, :], sin_ref[stream, :]
            )
            dkgain_ref[0:1, :] += key_gain_grad
            d_value = value_acc[stream, :]
            d_value = d_value + pltpu.roll(d_value, HEAD, 1)
            old_key = dk_ref[place, :].astype(jnp.float32)
            old_value = dv_ref[place, :].astype(jnp.float32)
            mine = half == which
            later = which > 0
            old_key = jnp.where(later, old_key, 0.0)
            old_value = jnp.where(later, old_value, 0.0)
            dk_ref[place, :] = jnp.where(mine, d_key, old_key).astype(dk_ref.dtype)
            dv_ref[place, :] = jnp.where(mine, d_value, old_value).astype(dv_ref.dtype)
            return carried

        lax.fori_loop(0, contexts * blocks, one, 0)


def attention(backward, contexts, qkv, cosine, sine, starts, gain_query, gain_key, d_attended):
    rows = qkv.shape[0]
    stream_blocks = rows // BLK
    blocks = stream_blocks // contexts
    window = min(MAXLEN + BLK, rows)
    pairs = QHEADS // contexts // 2
    dims = (contexts, blocks, window)

    def moving():
        return pl.BlockSpec((BLK, PAIR), lambda g, s: (arrival(s, contexts, blocks), g))

    def whole(shape, column=0):
        return pl.BlockSpec(shape, lambda g, s: (0, column))

    tall = (rows, PAIR)
    in_specs = [
        moving(),
        whole(tall, pairs),
        whole(tall, pairs + 1),
        whole(tall),
        whole(tall),
        whole((stream_blocks, BLK)),
        whole((1, PAIR)),
        whole((1, PAIR)),
    ]
    operands = [
        qkv,
        qkv,
        qkv,
        cosine,
        sine,
        starts,
        jnp.concatenate([gain_query, gain_query])[None, :],
        jnp.concatenate([gain_key, gain_key])[None, :],
    ]
    scratch = [pltpu.VMEM(tall, jnp.bfloat16), pltpu.VMEM(tall, jnp.bfloat16)]
    params = pltpu.CompilerParams(
        dimension_semantics=("arbitrary", "arbitrary"), vmem_limit_bytes=48 * 1024 * 1024
    )
    products = 2 * 2 * stream_blocks * BLK * window * PAIR * pairs
    if not backward:
        return pl.pallas_call(
            lambda *refs: forward_kernel(dims, *refs),
            grid=(pairs, stream_blocks),
            in_specs=in_specs,
            out_specs=moving(),
            out_shape=jax.ShapeDtypeStruct((rows, pairs * PAIR), jnp.bfloat16),
            scratch_shapes=scratch,
            compiler_params=params,
            cost_estimate=pl.CostEstimate(
                flops=2 * products, bytes_accessed=10 * rows * PAIR * 4, transcendentals=0
            ),
            name="attention_forward",
        )(*operands)
    accs = [pltpu.VMEM(tall, jnp.float32), pltpu.VMEM(tall, jnp.float32)]
    return pl.pallas_call(
        lambda *refs: backward_kernel(dims, *refs),
        grid=(pairs, stream_blocks),
        in_specs=in_specs + [moving()],
        out_specs=[moving(), whole(tall), whole(tall), whole((8, PAIR)), whole((8, PAIR))],
        out_shape=[
            jax.ShapeDtypeStruct((rows, pairs * PAIR), jnp.bfloat16),
            jax.ShapeDtypeStruct(tall, jnp.bfloat16),
            jax.ShapeDtypeStruct(tall, jnp.bfloat16),
            jax.ShapeDtypeStruct((8, PAIR), jnp.float32),
            jax.ShapeDtypeStruct((8, PAIR), jnp.float32),
        ],
        scratch_shapes=scratch + accs,
        compiler_params=params,
        cost_estimate=pl.CostEstimate(
            flops=5 * products, bytes_accessed=16 * rows * PAIR * 4, transcendentals=0
        ),
        name="attention_backward",
    )(*operands, d_attended)


def on_device(
    tokens,
    segments,
    attention_gain,
    query_weight,
    key_weight,
    value_weight,
    query_gain,
    key_gain,
    output_weight,
    feedforward_gain,
    gate_weight,
    up_weight,
    down_weight,
    cotangent,
):
    contexts = lax.axis_size("context")
    tensors = lax.axis_size("tensor")
    tok_rows = tokens.shape[0]
    group_rows = segments.shape[1]
    hidden = gate_weight.shape[1]
    width = tokens.shape[1]
    query_cols = query_weight.shape[1]
    kv_cols = key_weight.shape[1]
    qkv_cols = query_cols + 2 * kv_cols
    rows_axes = ("shard", "context")
    bfloat = jnp.bfloat16

    def shift(values, step):
        pairs = [(i, (i + step) % tensors) for i in range(tensors)]
        return lax.ppermute(values, "tensor", pairs)

    attn_local = jnp.concatenate([query_weight, key_weight, value_weight, output_weight], axis=1)
    attn_cols = lax.all_gather(attn_local, "tensor", axis=0)
    qkv_weight = lax.all_gather(attn_cols[:, :, :qkv_cols], rows_axes, axis=1, tiled=True)
    grad_rows = [cotangent] + [shift(cotangent, step) for step in range(1, tensors)]

    starts, cosine, sine = tables(segments[0])
    inputs_f32 = tokens.astype(jnp.float32)
    normed_f32, norm_in_pull = jax.vjp(rms_norm, inputs_f32, attention_gain)
    normed_in = normed_f32.astype(bfloat)

    qkv_weight, out_local, gate_local, up_local, down_local = lax.optimization_barrier(
        (qkv_weight, attn_cols[:, :, qkv_cols:], gate_weight, up_weight, down_weight)
    )
    out_weight = lax.all_gather(out_local, rows_axes, axis=1, tiled=True)
    pair_weight = lax.all_gather(
        jnp.concatenate([gate_local, up_local], axis=1), rows_axes, axis=0, tiled=True
    )
    down_full = lax.all_gather(down_local, rows_axes, axis=0, tiled=True)

    qkv_send = jnp.einsum(
        "md,tdn->tmn", normed_in, qkv_weight, preferred_element_type=jnp.float32
    ).astype(bfloat)
    qkv = lax.all_to_all(qkv_send, "context", split_axis=0, concat_axis=0, tiled=True)
    qkv = qkv.reshape(group_rows, qkv_cols)
    mixed = attention(
        False, contexts, qkv, cosine, sine, starts, query_gain, key_gain, None
    )
    mixed, *grad_rows = lax.optimization_barrier((mixed, *grad_rows))
    attended = lax.all_to_all(
        mixed.reshape(contexts, tok_rows, query_cols),
        "context",
        split_axis=0,
        concat_axis=0,
        tiled=True,
    )
    hidden_in = inputs_f32 + jnp.einsum(
        "tmk,tdk->md", attended, out_weight, preferred_element_type=jnp.float32
    )
    mid_f32, mid_pull = jax.vjp(rms_norm, hidden_in, feedforward_gain)
    normed_mid = mid_f32.astype(bfloat)
    normed_rows = [normed_mid] + [shift(normed_mid, step) for step in range(1, tensors)]

    outputs_part, grads_part = [], []
    pair_grad = down_grad = None
    for step in range(tensors):
        if step > 0:
            normed_rows[step], pair_grad, down_grad = lax.optimization_barrier(
                (normed_rows[step], pair_grad, down_grad)
            )
        pre = product(normed_rows[step], pair_weight)
        d_activated = product(grad_rows[step], down_full)
        gate_pre, up_pre = pre[:, :hidden], pre[:, hidden:]
        silu_gate, silu_slope = silu_parts(gate_pre)
        activated = (silu_gate * up_pre).astype(bfloat)
        d_gate = (d_activated * up_pre * silu_slope).astype(bfloat)
        d_up = (d_activated * silu_gate).astype(bfloat)
        d_pair = jnp.concatenate([d_gate, d_up], axis=1)
        d_mid = product_cols(d_pair, pair_weight)
        if step > 0:
            d_mid = shift(d_mid.astype(bfloat), -step).astype(jnp.float32)
        grads_part.append(d_mid)
        outputs_part.append(product_cols(activated, down_full))
        pair_term = product_rows(normed_rows[step], d_pair)
        down_term = product_rows(grad_rows[step], activated)
        pair_grad = pair_term if step == 0 else pair_grad + pair_term
        down_grad = down_term if step == 0 else down_grad + down_term
    pair_owned = lax.psum_scatter(
        pair_grad.astype(bfloat), rows_axes, scatter_dimension=0, tiled=True
    )
    down_owned = lax.psum_scatter(
        down_grad.astype(bfloat), rows_axes, scatter_dimension=0, tiled=True
    )
    d_normed_mid = sum(grads_part[1:], grads_part[0])
    d_normed_mid, *late = lax.optimization_barrier(
        (d_normed_mid, *[part.astype(bfloat) for part in outputs_part[1:]])
    )
    returned = [shift(late[step - 1], -step) for step in range(1, tensors)]

    d_hidden_mid, feedforward_gain_grad = mid_pull(d_normed_mid)
    d_hidden = cotangent.astype(jnp.float32) + d_hidden_mid
    d_branch = d_hidden.astype(bfloat)
    d_attended_send = jnp.einsum(
        "md,tdk->tmk", d_branch, out_weight, preferred_element_type=jnp.float32
    ).astype(bfloat)
    d_attended = lax.all_to_all(
        d_attended_send, "context", split_axis=0, concat_axis=0, tiled=True
    ).reshape(group_rows, query_cols)
    out_grad = jnp.einsum(
        "md,tmk->tdk", d_branch, attended, preferred_element_type=jnp.float32
    ).astype(bfloat)
    out_rows = lax.psum_scatter(out_grad, rows_axes, scatter_dimension=1, tiled=True)

    d_query_here, d_key_here, d_value_here, query_gain_rows, key_gain_rows = attention(
        True, contexts, qkv, cosine, sine, starts, query_gain, key_gain, d_attended
    )
    d_query_here, d_key_here, d_value_here, *returned = lax.optimization_barrier(
        (d_query_here, d_key_here, d_value_here, *returned)
    )
    ffn_output = outputs_part[0]
    for part in returned:
        ffn_output = ffn_output + part.astype(jnp.float32)
    block_output = hidden_in + ffn_output
    query_gain_grad = query_gain_rows[0, :HEAD] + query_gain_rows[0, HEAD:]
    key_gain_grad = key_gain_rows[0, :HEAD]
    d_qkv_send = jnp.concatenate([d_query_here, d_key_here, d_value_here], axis=1)
    d_qkv = lax.all_to_all(
        d_qkv_send.reshape(contexts, tok_rows, qkv_cols),
        "context",
        split_axis=0,
        concat_axis=0,
        tiled=True,
    )
    qkv_grad = jnp.einsum(
        "md,tmn->tdn", normed_in, d_qkv, preferred_element_type=jnp.float32
    ).astype(bfloat)
    qkv_grad, pair_owned, down_owned, out_rows = lax.optimization_barrier(
        (qkv_grad, pair_owned, down_owned, out_rows)
    )
    qkv_rows = lax.psum_scatter(qkv_grad, rows_axes, scatter_dimension=1, tiled=True)
    d_normed_in = jnp.einsum(
        "tmn,tdn->md", d_qkv, qkv_weight, preferred_element_type=jnp.float32
    )
    d_inputs_norm, attention_gain_grad = norm_in_pull(d_normed_in)
    token_grad = d_hidden + d_inputs_norm
    attn_owned = lax.psum_scatter(
        jnp.concatenate([qkv_rows, out_rows], axis=2), "tensor", scatter_dimension=0, tiled=True
    )[0].astype(jnp.float32)
    gains = jnp.concatenate(
        [attention_gain_grad, feedforward_gain_grad, query_gain_grad, key_gain_grad]
    )
    gains = gains.reshape(-1, PAIR)
    for axis in ("shard", "context", "tensor"):
        size = lax.axis_size(axis)
        reach = 1
        while reach < size:
            gains = gains + lax.ppermute(gains, axis, [(i, i ^ reach) for i in range(size)])
            reach *= 2
    gains = gains.reshape(-1)
    pair_owned = pair_owned.astype(jnp.float32)
    return (
        block_output,
        token_grad,
        gains[:width],
        attn_owned[:, :query_cols],
        attn_owned[:, query_cols : query_cols + kv_cols],
        attn_owned[:, query_cols + kv_cols : qkv_cols],
        gains[2 * width : 2 * width + HEAD],
        gains[2 * width + HEAD :],
        attn_owned[:, qkv_cols:],
        gains[width : 2 * width],
        pair_owned[:, :hidden],
        pair_owned[:, hidden:],
        down_owned.astype(jnp.float32),
    )


def solution(mesh):
    placed = (
        P(("shard", "context", "tensor"), None),
        P(("shard", "tensor"), None),
        P(),
        P(("shard", "context"), "tensor"),
        P(("shard", "context"), "tensor"),
        P(("shard", "context"), "tensor"),
        P(),
        P(),
        P(("shard", "context"), "tensor"),
        P(),
        P(("shard", "context"), "tensor"),
        P(("shard", "context"), "tensor"),
        P(("shard", "context"), "tensor"),
        P(("shard", "context", "tensor"), None),
    )
    return jax.shard_map(
        on_device,
        mesh=mesh,
        in_specs=placed,
        out_specs=(
            P(("shard", "context", "tensor"), None),
            P(("shard", "context", "tensor"), None),
            P(),
            P(("shard", "context"), "tensor"),
            P(("shard", "context"), "tensor"),
            P(("shard", "context"), "tensor"),
            P(),
            P(),
            P(("shard", "context"), "tensor"),
            P(),
            P(("shard", "context"), "tensor"),
            P(("shard", "context"), "tensor"),
            P(("shard", "context"), "tensor"),
        ),
        check_vma=False,
    )
```
